32 devices in a mesh: frag: 2 (over x), aux: 16 (over z, y, core).
Axes of the slice: x: 2, y: 2, z: 4, core: 2. Of those that a mesh axis runs over, the one named last changes fastest.
Arguments:
- three_index: bfloat16 [512, 8, 128, 128], P(('frag', 'aux')), parts along dimension 0, may hold values from -0.125 to 0.125
- slab_blocks: int32 [512], P(('frag', 'aux')), parts along dimension 0, may hold values from 0 to 255
- slab_count: int32 [32], P(('frag', 'aux')), parts along dimension 0, may hold values from 1 to 16, 128 in all
- pair_mask: int32 [32, 16], P('frag'), parts along dimension 0, may hold values 0 or 1
- coeffs: bfloat16 [4096, 200], P(('frag', 'aux')), parts along dimension 0, may hold values from -1 to 1
Outputs:
- exchange: float32 [4096, 2048], P(('frag', 'aux')), parts along dimension 0
The draws below stay inside these ranges and needn't reach their ends.
There are 2 independent parts, one for each index of `frag`. The reference program is written for one: setup_inputs(seed, part) draws one part's arguments, and reference() takes and returns one part's arrays. A program takes and returns all parts, laid end to end along the dimension named above; each array names one. Nothing has to cross between parts.
Inputs may be any that keep to these rules, and one draw needn't show every extreme that they name: `slab_count`: each slab has 1 to 16 live slots; some slab has exactly 16; within each fragment the counts sum to 128. `slab_blocks`: slots past a slab's count carry values that do not count; a block pair may stand in several slots of a slab.
All inputs are finite; a program needn't handle non-finite values. No bound on the sum of `slab_count` on one device may be relied on, other than what follows from the above.
Results may differ from the reference program's by a relative error of at most 0.0012.
Values may be sent and summed in bfloat16 or wider, within the bound.
A program may use at most 128 MiB of HBM per device.

```python
import math
import jax
import jax.numpy as jnp
import numpy as np
from jax import lax

NB = 16
BS = 128
NOCC = 200
P_DEV = 8
NNZ = 16
NAO = 2048
NAUX = 128
SLOTS = 256
N_AUX = 16


def set_ends(result, rng, least, top_value):
    spot = [jax.random.randint(jax.random.fold_in(rng, axis), (), 0, length) for axis, length in enumerate(result.shape)]
    widest = result.shape.index(max(result.shape))
    next_to = spot[:widest] + [(spot[widest] + 1) % result.shape[widest]] + spot[widest + 1:]
    return result.at[tuple(spot)].set(least).at[tuple(next_to)].set(top_value)


def steps_of(stream_key, shape, shards, low, high):
    loudness = 1.0
    for axis_at, shards_of in shards:
        draws = jax.random.uniform(jax.random.fold_in(jax.random.fold_in(stream_key, 6), axis_at), (shards_of,), jnp.float32, low / len(shards), high / len(shards))
        loudness = loudness * jnp.repeat(jnp.exp(draws), shape[axis_at] // shards_of).reshape((-1,) + (1,) * (len(shape) - 1 - axis_at))
    return loudness


def split_up(count, total, bound, slope):
    portions = [(1 << 20) // math.isqrt(standing ** slope) + 1 for standing in range(2, count + 1)]
    rest, holding = total - bound - (count - 1), [1] * (count - 1)
    while rest > 0:
        candidates = [i for i in range(count - 1) if holding[i] < bound]
        mass, remaining = sum([portions[i] for i in candidates]), rest
        for i in candidates:
            extra = min(bound - holding[i], max(1, remaining * portions[i] // mass), rest)
            holding[i] = holding[i] + extra
            rest = rest - extra
    return np.array([bound] + holding)


def ragged(own_key, count, total, bound, skew):
    if count == 2:
        one = jax.random.randint(own_key, (), max(1, total - bound), min(bound, total - 1) + 1)
        return jnp.stack([one, total - one])
    sizes = jnp.asarray(split_up(count, total, bound, skew), jnp.int32)
    couples = (count - 1) // 2
    giver, sink = sizes[1:1 + 2 * couples:2], sizes[2:2 + 2 * couples:2]
    room = jnp.minimum(giver - 1, bound - sink)
    passed = jax.random.randint(jax.random.fold_in(own_key, 1), (couples,), 0, 1 << 20) % (room + 1)
    sizes = sizes.at[1:1 + 2 * couples:2].set(giver - passed).at[2:2 + 2 * couples:2].set(sink + passed)
    return sizes[jax.random.permutation(jax.random.fold_in(own_key, 2), count)]


def gaussian(own_key, shape, deviation, reach, cuts=(), held_as=jnp.bfloat16):
    level = steps_of(own_key, shape, cuts, -0.22, 0.18) if cuts else 1.0
    values = jax.random.normal(own_key, shape, jnp.float32) * deviation * level
    return jnp.minimum(jnp.maximum(values, -reach), reach).astype(held_as)


def setup_inputs(seed: int = 0, part: int = 0) -> dict:
    splits = jax.random.split(jax.random.key(seed), 6)
    part_splits = jax.random.split(jax.random.fold_in(splits[5], part), 6)
    return {
        "three_index": gaussian(part_splits[0], (SLOTS, P_DEV, BS, BS), ((BS * NAUX) ** -0.5), 0.125, ((0, 16),)),
        "slab_blocks": set_ends(jax.random.randint(part_splits[1], (SLOTS,), 0, NB * NB), jax.random.fold_in(part_splits[1], 1), 0, (NB * NB) - 1).astype(jnp.int32),
        "slab_count": ragged(part_splits[2], N_AUX, N_AUX * NNZ // 2, NNZ, 2).astype(jnp.int32),
        "pair_mask": set_ends((jax.random.randint(part_splits[3], (NB, NB), 0, 4) < 3).astype(jnp.int32), jax.random.fold_in(part_splits[3], 1), 0, 1),
        "coeffs": gaussian(part_splits[4], (NAO, NOCC), (NOCC ** -0.5), 1.0, ((0, 16),)),
    }


def reference(three_index, slab_blocks, slab_count, pair_mask, coeffs):
    highest = lax.Precision.HIGHEST
    cblocks = coeffs.reshape(NB, BS, NOCC).astype(jnp.float32)
    block_ids = jnp.arange(NB, dtype=jnp.int32)
    slot_ids = jnp.arange(NNZ, dtype=jnp.int32)

    def add_slab(slab_index, total):
        slab_index = slab_index.astype(jnp.int32)
        first_slot = (slab_index * NNZ).astype(jnp.int32)
        values = lax.dynamic_slice_in_dim(three_index, first_slot, NNZ, 0).astype(jnp.float32)
        pair_ids = lax.dynamic_slice_in_dim(slab_blocks, first_slot, NNZ, 0)
        row_block = pair_ids // NB
        col_block = pair_ids % NB
        usable = (slot_ids < slab_count[slab_index]) & (pair_mask[row_block, col_block] == 1)
        chosen = jnp.take(cblocks, col_block, axis=0)
        halfway = jnp.einsum("kprl,kli->kpri", values, chosen, precision=highest)
        weights = ((row_block[:, None] == block_ids[None, :]) & usable[:, None]).astype(jnp.float32)
        fitted = jnp.einsum("kb,kpri->brpi", weights, halfway, precision=highest)
        factor = fitted.reshape(NB * BS, P_DEV * NOCC).astype(jnp.bfloat16)
        factor = lax.optimization_barrier(factor).astype(jnp.float32)
        return total + jnp.dot(factor, factor.T, precision=highest)

    return lax.fori_loop(0, N_AUX, add_slab, jnp.zeros((NB * BS, NB * BS), jnp.float32))
```

```python
import functools

import jax
import jax.numpy as jnp
from jax import lax
from jax.experimental import pallas as pl
from jax.experimental.pallas import tpu as pltpu
from jax.sharding import PartitionSpec as P

MESH = pl.DeviceIdType.MESH
VMEM_BYTES = 56 * 1024 * 1024
TOP = 32000.0
TINY = 1e-37
LANES = 256


def flip(value, bits):
    return sum(((value >> j) & 1) << (bits - 1 - j) for j in range(bits))


def slab_kernel(blocks, count, mask, t_ref, c_ref, q_ref, m_ref, total, factor, seen, *, slots, width, split):
    g = pl.program_id(0)
    nb, size, _ = c_ref.shape
    aux = t_ref.shape[1]
    chunks = q_ref.shape[0]
    per = width // chunks
    rows = size // split

    @pl.when(g == 0)
    def _():
        for r in range(nb):
            seen[r] = 0
        m_ref[...] = jnp.zeros_like(m_ref)

    @pl.when(g < slots)
    def _():
        pair = blocks[g]
        row, col = pair // nb, pair % nb
        live = (g < count[0]) & (mask[row, col] == 1)

        @pl.when(live)
        def _():
            part = jnp.dot(t_ref[0].reshape(aux * size, size), c_ref[col], preferred_element_type=jnp.float32)
            before = seen[row]

            @pl.when(before == 0)
            def _():
                total[row] = part

            @pl.when(before != 0)
            def _():
                total[row] += part

            seen[row] = 1

    @pl.when(g == slots)
    def _():
        @pl.loop(0, nb)
        def _(r):
            @pl.when(seen[r] != 0)
            def _():
                for p in range(aux):
                    factor[r, :, p * LANES:(p + 1) * LANES] = total[r, p * size:(p + 1) * size].astype(jnp.bfloat16)

            @pl.when(seen[r] == 0)
            def _():
                factor[r] = jnp.zeros(factor.shape[1:], factor.dtype)

            @pl.when(r < width - 1)
            def _():
                factor[nb + r] = factor[r]

    @pl.when(g >= slots)
    def _():
        r = g - slots

        @pl.when(seen[r] != 0)
        def _():
            for c in range(chunks):
                right = factor[pl.ds(r + c * per, per)].reshape(per * size, factor.shape[2])
                value = lax.dot_general(factor[r], right, (((1,), (1,)), ((), ())), preferred_element_type=jnp.float32)
                for h in range(split):
                    q_ref[c, flip(h, split.bit_length() - 1), 0] = value[h * rows:(h + 1) * rows]
                if c == 0:
                    m_ref[...] = jnp.maximum(m_ref[...], jnp.max(jnp.abs(value[:, :size])))

        @pl.when(seen[r] == 0)
        def _():
            q_ref[...] = jnp.zeros_like(q_ref)


def encode(value, inverse):
    root = jnp.sqrt(jnp.abs(value) * inverse) * TOP + 0.5
    return jnp.where(value < 0, -root, root).astype(jnp.int16)


def decode(code, scale):
    value = code.astype(jnp.float32)
    return value * jnp.abs(value) * scale


def reduce_kernel(q_ref, m_ref, out_ref, acc, snd, rcv, s_m, r_m, m_snd, m_rcv, send_sem, recv_sem, sm_send, sm_recv, mir_send, mir_recv, *, n, nb, width, mirrored):
    chunks, _, rows, cw = q_ref.shape
    size = out_ref.shape[1] // nb
    per = width // chunks
    stages = n.bit_length() - 1
    me = lax.axis_index("aux")
    r = me // (n // nb)
    bit = [(me // (1 << k)) % 2 for k in range(stages)]
    partner = [me + (1 << k) * (1 - 2 * bit[k]) for k in range(stages)]
    counts = [n >> (k + 1) for k in range(stages)]
    starts = [n - (n >> k) for k in range(stages)]
    mirror = list(range(1, width - 1)) if mirrored else []

    barrier = pltpu.get_barrier_semaphore()
    if mirrored:
        peers = [lax.rem(me + d, n) for d in range(1, n)]
    else:
        peers = partner
    for peer in peers:
        pl.semaphore_signal(barrier, inc=1, device_id={"aux": peer}, device_id_type=MESH)
    pl.semaphore_wait(barrier, len(peers))

    def scale_copy(k):
        return pltpu.make_async_remote_copy(
            src_ref=s_m.at[k], dst_ref=r_m.at[k], send_sem=sm_send.at[k], recv_sem=sm_recv.at[k],
            device_id={"aux": partner[k]}, device_id_type=MESH)

    def data_copy(k, c):
        span = pl.ds(starts[k], counts[k])
        return pltpu.make_async_remote_copy(
            src_ref=snd.at[c, span], dst_ref=rcv.at[c, span], send_sem=send_sem.at[k, c], recv_sem=recv_sem.at[k, c],
            device_id={"aux": partner[k]}, device_id_type=MESH)

    def mirror_copy(d):
        return pltpu.make_async_remote_copy(
            src_ref=m_snd.at[d], dst_ref=m_rcv.at[d], send_sem=mir_send.at[d], recv_sem=mir_recv.at[d],
            device_id={"aux": lax.rem(me + d, n)}, device_id_type=MESH)

    def place(block, value):
        out_ref[:, pl.ds(pl.multiple_of(block * size, size), size)] = value

    def before(k, c, j):
        return q_ref[c, bit[0] * counts[0] + j] if k == 1 else acc[c, j]

    def event(k, c):
        if k == 0:
            if c == 0:
                s_m[0] = jnp.maximum(m_ref[...], TINY)
                scale_copy(0).start()
            inverse = 1.0 / s_m[0, 0:1]

            @pl.loop(0, counts[0])
            def _(j):
                snd[c, j] = encode(q_ref[c, (1 - bit[0]) * counts[0] + j], inverse)

            data_copy(0, c).start()
            return
        if c == 0:
            scale_copy(k - 1).wait_recv()
            if k < stages:
                s_m[k] = s_m[k - 1] + r_m[k - 1]
                scale_copy(k).start()
        back = r_m[k - 1, 0:1] * (1.0 / (TOP * TOP))
        data_copy(k - 1, c).wait_recv()
        if k < stages:
            inverse = 1.0 / s_m[k, 0:1]

            @pl.loop(0, counts[k])
            def _(j):
                i = (1 - bit[k]) * counts[k] + j
                value = before(k, c, i) + decode(rcv[c, starts[k - 1] + i], back)
                snd[c, starts[k] + j] = encode(value, inverse)

            data_copy(k, c).start()

            @pl.loop(0, counts[k])
            def _(j):
                i = bit[k] * counts[k] + j
                acc[c, j] = before(k, c, i) + decode(rcv[c, starts[k - 1] + i], back)

            return
        value = acc[c, 0] + decode(rcv[c, starts[k - 1]], back)
        for i in range(per):
            d = c * per + i
            block = value[:, i * size:(i + 1) * size]
            if d in mirror:
                m_snd[d] = block.T
                mirror_copy(d).start()
            place(lax.rem(r + d, nb), block)

    for t in range(chunks + stages):
        for c in range(chunks):
            if 0 <= t - c <= stages:
                event(t - c, c)
    for d in mirror:
        mirror_copy(d).wait_recv()
        place(lax.rem(r + nb - d, nb), m_rcv[d])
    for k in range(stages):
        scale_copy(k).wait_send()
        for c in range(chunks):
            data_copy(k, c).wait_send()
    for d in mirror:
        mirror_copy(d).wait_send()


def per_device(n, three_index, slab_blocks, slab_count, pair_mask, coeffs):
    slots, aux, size, _ = three_index.shape
    nb = pair_mask.shape[0]
    mirrored = n == nb
    split = n // nb
    width = nb // 2 + 1 if mirrored else nb
    per = max(d for d in range(1, 5) if width % d == 0)
    chunks, cw, rows = width // per, per * size, size // split
    bits = nb.bit_length() - 1
    stages = n.bit_length() - 1
    padded = jnp.pad(coeffs, ((0, 0), (0, LANES - coeffs.shape[1])))
    gathered = lax.all_gather(padded, "aux", axis=0, tiled=True).reshape(nb, size, LANES)

    q, m = pl.pallas_call(
        functools.partial(slab_kernel, slots=slots, width=width, split=split),
        grid_spec=pltpu.PrefetchScalarGridSpec(
            num_scalar_prefetch=3,
            grid=(slots + nb,),
            in_specs=[
                pl.BlockSpec((1, aux, size, size), lambda g, *_: (jnp.minimum(g, slots - 1), 0, 0, 0)),
                pl.BlockSpec((nb, size, LANES), lambda g, *_: (0, 0, 0)),
            ],
            out_specs=[
                pl.BlockSpec((chunks, split, 1, rows, cw), lambda g, *_: (0, 0, flip(jnp.maximum(g - slots, 0), bits), 0, 0)),
                pl.BlockSpec((8, cw), lambda g, *_: (0, 0)),
            ],
            scratch_shapes=[
                pltpu.VMEM((nb, aux * size, LANES), jnp.float32),
                pltpu.VMEM((nb + width - 1, size, aux * LANES), jnp.bfloat16),
                pltpu.SMEM((nb,), jnp.int32),
            ],
        ),
        out_shape=[
            jax.ShapeDtypeStruct((chunks, split, nb, rows, cw), jnp.float32),
            jax.ShapeDtypeStruct((8, cw), jnp.float32),
        ],
        compiler_params=pltpu.CompilerParams(vmem_limit_bytes=VMEM_BYTES, dimension_semantics=("arbitrary",)),
    )(slab_blocks, slab_count, pair_mask, three_index, gathered)

    return pl.pallas_call(
        functools.partial(reduce_kernel, n=n, nb=nb, width=width, mirrored=mirrored),
        out_shape=jax.ShapeDtypeStruct((rows, nb * size), jnp.float32),
        in_specs=[pl.BlockSpec(memory_space=pltpu.VMEM)] * 2,
        out_specs=pl.BlockSpec(memory_space=pltpu.VMEM),
        scratch_shapes=[
            pltpu.VMEM((chunks, n // 4, rows, cw), jnp.float32),
            pltpu.VMEM((chunks, n, rows, cw), jnp.int16),
            pltpu.VMEM((chunks, n, rows, cw), jnp.int16),
            pltpu.VMEM((stages, 8, cw), jnp.float32),
            pltpu.VMEM((stages, 8, cw), jnp.float32),
            pltpu.VMEM((width, size, size), jnp.float32),
            pltpu.VMEM((width, size, size), jnp.float32),
            pltpu.SemaphoreType.DMA((stages, chunks)),
            pltpu.SemaphoreType.DMA((stages, chunks)),
            pltpu.SemaphoreType.DMA((stages,)),
            pltpu.SemaphoreType.DMA((stages,)),
            pltpu.SemaphoreType.DMA((width,)),
            pltpu.SemaphoreType.DMA((width,)),
        ],
        compiler_params=pltpu.CompilerParams(collective_id=0, has_side_effects=True, vmem_limit_bytes=VMEM_BYTES),
    )(q.reshape(chunks, n, rows, cw), m)


def solution(mesh):
    return jax.shard_map(
        functools.partial(per_device, mesh.shape["aux"]),
        mesh=mesh,
        in_specs=(
            P(("frag", "aux"), None, None, None),
            P(("frag", "aux")),
            P(("frag", "aux")),
            P("frag", None),
            P(("frag", "aux"), None),
        ),
        out_specs=P(("frag", "aux"), None),
        check_vma=False,
    )
```

```python
import functools

import jax
import jax.numpy as jnp
from jax import lax
from jax.experimental import pallas as pl
from jax.experimental.pallas import tpu as pltpu
from jax.sharding import PartitionSpec as P

MESH = pl.DeviceIdType.MESH
VMEM_BYTES = 56 * 1024 * 1024
TOP = 32000.0
TINY = 1e-37
LANES = 256


def flip(value, bits):
    return sum(((value >> j) & 1) << (bits - 1 - j) for j in range(bits))


def partners_of(me, stages):
    return [me + (1 << k) * (1 - 2 * ((me // (1 << k)) % 2)) for k in range(stages)]


def gather_kernel(c_ref, g_ref, send_sem, recv_sem, *, n):
    stages = n.bit_length() - 1
    me = lax.axis_index("aux")
    partner = partners_of(me, stages)
    barrier = pltpu.get_barrier_semaphore()
    for peer in partner:
        pl.semaphore_signal(barrier, inc=1, device_id={"aux": peer}, device_id_type=MESH)
    g_ref[me] = jnp.zeros(g_ref.shape[1:], g_ref.dtype)
    g_ref[me, :, 0:c_ref.shape[0]] = c_ref[...].T
    pl.semaphore_wait(barrier, stages)

    def copy(x, k):
        unit = me + sum(partner[j] - me for j in range(stages) if (x >> j) & 1)
        return pltpu.make_async_remote_copy(
            src_ref=g_ref.at[unit], dst_ref=g_ref.at[unit], send_sem=send_sem.at[x, k], recv_sem=recv_sem.at[x ^ (1 << k)],
            device_id={"aux": partner[k]}, device_id_type=MESH)

    started = []
    for x in sorted(range(n), key=lambda x: (x.bit_count(), -x)):
        low = stages if x == 0 else (x & -x).bit_length() - 1
        if x:
            copy(x ^ (1 << low), low).wait_recv()
        for k in reversed(range(low)):
            started.append(copy(x, k))
            started[-1].start()
    for one in started:
        one.wait_send()


def slab_kernel(blocks, count, mask, t_ref, c_ref, q_ref, m_ref, total, factor, seen, *, slots, width, split):
    g = pl.program_id(0)
    nb, size, _ = c_ref.shape
    aux = t_ref.shape[1]
    chunks, cw = q_ref.shape[0], q_ref.shape[4]
    group = max(d for d in range(1, 5) if width % d == 0)
    per = cw // size
    rows = size // split

    @pl.when(g == 0)
    def _():
        for r in range(nb):
            seen[r] = 0
        m_ref[...] = jnp.zeros_like(m_ref)

    @pl.when(g < slots)
    def _():
        pair = blocks[g]
        row, col = pair // nb, pair % nb
        live = (g < count[0]) & (mask[row, col] == 1)

        @pl.when(live)
        def _():
            part = jnp.dot(t_ref[0].reshape(aux * size, size), c_ref[col], preferred_element_type=jnp.float32)
            before = seen[row]

            @pl.when(before == 0)
            def _():
                total[row] = part

            @pl.when(before != 0)
            def _():
                total[row] += part

            seen[row] = 1

    @pl.when(g == slots)
    def _():
        @pl.loop(0, nb)
        def _(r):
            @pl.when(seen[r] != 0)
            def _():
                for p in range(aux):
                    factor[r, :, p * LANES:(p + 1) * LANES] = total[r, p * size:(p + 1) * size].astype(jnp.bfloat16)

            @pl.when(seen[r] == 0)
            def _():
                factor[r] = jnp.zeros(factor.shape[1:], factor.dtype)

            @pl.when(r < width - 1)
            def _():
                factor[nb + r] = factor[r]

    @pl.when(g >= slots)
    def _():
        r = g - slots

        @pl.when(seen[r] != 0)
        def _():
            for d in range(0, width, group):
                right = factor[pl.ds(r + d, group)].reshape(group * size, factor.shape[2])
                value = lax.dot_general(factor[r], right, (((1,), (1,)), ((), ())), preferred_element_type=jnp.float32)
                for h in range(split):
                    for i in range(0, group, per):
                        q_ref[(d + i) // per, flip(h, split.bit_length() - 1), 0] = value[h * rows:(h + 1) * rows, i * size:(i + per) * size]
                if d == 0:
                    m_ref[...] = jnp.maximum(m_ref[...], jnp.max(jnp.abs(value[:, :size])))

        @pl.when(seen[r] == 0)
        def _():
            q_ref[...] = jnp.zeros_like(q_ref)


def encode(value, inverse):
    root = jnp.sqrt(jnp.abs(value) * inverse) * TOP + 0.5
    return jnp.where(value < 0, -root, root).astype(jnp.int16)


def decode(code, scale):
    value = code.astype(jnp.float32)
    return value * jnp.abs(value) * scale


def reduce_kernel(q_ref, m_ref, out_ref, acc, snd, rcv, s_m, r_m, m_snd, m_rcv, send_sem, recv_sem, sm_send, sm_recv, mir_send, mir_recv, *, n, nb, width, mirrored):
    chunks, _, rows, cw = q_ref.shape
    size = out_ref.shape[1] // nb
    per = width // chunks
    stages = n.bit_length() - 1
    me = lax.axis_index("aux")
    r = me // (n // nb)
    bit = [(me // (1 << k)) % 2 for k in range(stages)]
    partner = partners_of(me, stages)
    counts = [n >> (k + 1) for k in range(stages)]
    starts = [n - (n >> k) for k in range(stages)]
    steps = [min(4, count) for count in counts]
    mirror = list(range(1, width - 1)) if mirrored else []

    barrier = pltpu.get_barrier_semaphore()
    if mirrored:
        peers = [lax.rem(me + d, n) for d in range(1, n)]
    else:
        peers = partner
    for peer in peers:
        pl.semaphore_signal(barrier, inc=1, device_id={"aux": peer}, device_id_type=MESH)
    pl.semaphore_wait(barrier, len(peers))

    def scale_copy(k):
        return pltpu.make_async_remote_copy(
            src_ref=s_m.at[k], dst_ref=r_m.at[k], send_sem=sm_send.at[k], recv_sem=sm_recv.at[k],
            device_id={"aux": partner[k]}, device_id_type=MESH)

    def data_copy(k, c):
        span = pl.ds(starts[k], counts[k])
        return pltpu.make_async_remote_copy(
            src_ref=snd.at[c, span], dst_ref=rcv.at[c, span], send_sem=send_sem.at[k, c], recv_sem=recv_sem.at[k, c],
            device_id={"aux": partner[k]}, device_id_type=MESH)

    def mirror_copy(d):
        return pltpu.make_async_remote_copy(
            src_ref=m_snd.at[d], dst_ref=m_rcv.at[d], send_sem=mir_send.at[d], recv_sem=mir_recv.at[d],
            device_id={"aux": lax.rem(me + d, n)}, device_id_type=MESH)

    def place(block, value):
        out_ref[:, pl.ds(pl.multiple_of(block * size, size), size)] = value

    def before(k, c, j):
        return q_ref[c, pl.ds(bit[0] * counts[0] + j, steps[k])] if k == 1 else acc[c, pl.ds(j, steps[k])]

    def event(k, c):
        if k == 0:
            if c == 0:
                s_m[0] = jnp.maximum(m_ref[...], TINY)
                scale_copy(0).start()
            inverse = 1.0 / s_m[0, 0:1]

            @pl.loop(0, counts[0], step=steps[0])
            def _(j):
                snd[c, pl.ds(j, steps[0])] = encode(q_ref[c, pl.ds((1 - bit[0]) * counts[0] + j, steps[0])], inverse)

            data_copy(0, c).start()
            return
        if c == 0:
            scale_copy(k - 1).wait_recv()
            if k < stages:
                s_m[k] = s_m[k - 1] + r_m[k - 1]
                scale_copy(k).start()
        back = r_m[k - 1, 0:1] * (1.0 / (TOP * TOP))
        data_copy(k - 1, c).wait_recv()
        if k < stages:
            inverse = 1.0 / s_m[k, 0:1]

            @pl.loop(0, counts[k], step=steps[k])
            def _(j):
                i = (1 - bit[k]) * counts[k] + j
                value = before(k, c, i) + decode(rcv[c, pl.ds(starts[k - 1] + i, steps[k])], back)
                snd[c, pl.ds(starts[k] + j, steps[k])] = encode(value, inverse)

            data_copy(k, c).start()

            @pl.loop(0, counts[k], step=steps[k])
            def _(j):
                i = bit[k] * counts[k] + j
                acc[c, pl.ds(j, steps[k])] = before(k, c, i) + decode(rcv[c, pl.ds(starts[k - 1] + i, steps[k])], back)

            return
        value = acc[c, 0] + decode(rcv[c, starts[k - 1]], back)
        for i in range(per):
            d = c * per + i
            block = value[:, i * size:(i + 1) * size]
            if d in mirror:
                m_snd[d] = block.T
                mirror_copy(d).start()
            place(lax.rem(r + d, nb), block)

    def due(k, c):
        return (0.5 * c + 1.7 * k if k < 2 else 3.2 + 2.6 * (c + 1) + 2.5 * (k - 2), k, c)

    for k, c in sorted(((k, c) for k in range(stages + 1) for c in range(chunks)), key=lambda e: due(*e)):
        event(k, c)
    for d in mirror:
        mirror_copy(d).wait_recv()
        place(lax.rem(r + nb - d, nb), m_rcv[d])
    for k in range(stages):
        scale_copy(k).wait_send()
        for c in range(chunks):
            data_copy(k, c).wait_send()
    for d in mirror:
        mirror_copy(d).wait_send()


def per_device(n, three_index, slab_blocks, slab_count, pair_mask, coeffs):
    slots, aux, size, _ = three_index.shape
    nb = pair_mask.shape[0]
    mirrored = n == nb
    split = n // nb
    width = nb // 2 + 1 if mirrored else nb
    per = 1 if mirrored else 2
    chunks, cw, rows = width // per, per * size, size // split
    bits = nb.bit_length() - 1
    stages = n.bit_length() - 1
    gathered = pl.pallas_call(
        functools.partial(gather_kernel, n=n),
        out_shape=jax.ShapeDtypeStruct((n, rows, LANES), coeffs.dtype),
        in_specs=[pl.BlockSpec(memory_space=pltpu.VMEM)],
        out_specs=pl.BlockSpec(memory_space=pltpu.VMEM),
        scratch_shapes=[pltpu.SemaphoreType.DMA((n, stages)), pltpu.SemaphoreType.DMA((n,))],
        compiler_params=pltpu.CompilerParams(collective_id=1, has_side_effects=True, vmem_limit_bytes=VMEM_BYTES),
    )(coeffs.T).reshape(nb, size, LANES)

    q, m = pl.pallas_call(
        functools.partial(slab_kernel, slots=slots, width=width, split=split),
        grid_spec=pltpu.PrefetchScalarGridSpec(
            num_scalar_prefetch=3,
            grid=(slots + nb,),
            in_specs=[
                pl.BlockSpec((1, aux, size, size), lambda g, *_: (jnp.minimum(g, slots - 1), 0, 0, 0)),
                pl.BlockSpec((nb, size, LANES), lambda g, *_: (0, 0, 0)),
            ],
            out_specs=[
                pl.BlockSpec((chunks, split, 1, rows, cw), lambda g, *_: (0, 0, flip(jnp.maximum(g - slots, 0), bits), 0, 0)),
                pl.BlockSpec((8, cw), lambda g, *_: (0, 0)),
            ],
            scratch_shapes=[
                pltpu.VMEM((nb, aux * size, LANES), jnp.float32),
                pltpu.VMEM((nb + width - 1, size, aux * LANES), jnp.bfloat16),
                pltpu.SMEM((nb,), jnp.int32),
            ],
        ),
        out_shape=[
            jax.ShapeDtypeStruct((chunks, split, nb, rows, cw), jnp.float32),
            jax.ShapeDtypeStruct((8, cw), jnp.float32),
        ],
        compiler_params=pltpu.CompilerParams(vmem_limit_bytes=VMEM_BYTES, dimension_semantics=("arbitrary",)),
    )(slab_blocks, slab_count, pair_mask, three_index, gathered)

    return pl.pallas_call(
        functools.partial(reduce_kernel, n=n, nb=nb, width=width, mirrored=mirrored),
        out_shape=jax.ShapeDtypeStruct((rows, nb * size), jnp.float32),
        in_specs=[pl.BlockSpec(memory_space=pltpu.VMEM)] * 2,
        out_specs=pl.BlockSpec(memory_space=pltpu.VMEM),
        scratch_shapes=[
            pltpu.VMEM((chunks, n // 4, rows, cw), jnp.float32),
            pltpu.VMEM((chunks, n, rows, cw), jnp.int16),
            pltpu.VMEM((chunks, n, rows, cw), jnp.int16),
            pltpu.VMEM((stages, 8, cw), jnp.float32),
            pltpu.VMEM((stages, 8, cw), jnp.float32),
            pltpu.VMEM((width, size, size), jnp.float32),
            pltpu.VMEM((width, size, size), jnp.float32),
            pltpu.SemaphoreType.DMA((stages, chunks)),
            pltpu.SemaphoreType.DMA((stages, chunks)),
            pltpu.SemaphoreType.DMA((stages,)),
            pltpu.SemaphoreType.DMA((stages,)),
            pltpu.SemaphoreType.DMA((width,)),
            pltpu.SemaphoreType.DMA((width,)),
        ],
        compiler_params=pltpu.CompilerParams(collective_id=0, has_side_effects=True, vmem_limit_bytes=VMEM_BYTES),
    )(q.reshape(chunks, n, rows, cw), m)


def solution(mesh):
    return jax.shard_map(
        functools.partial(per_device, mesh.shape["aux"]),
        mesh=mesh,
        in_specs=(
            P(("frag", "aux"), None, None, None),
            P(("frag", "aux")),
            P(("frag", "aux")),
            P("frag", None),
            P(("frag", "aux"), None),
        ),
        out_specs=P(("frag", "aux"), None),
        check_vma=False,
    )
```

```python
import functools

import jax
import jax.numpy as jnp
from jax import lax
from jax.experimental import pallas as pl
from jax.experimental.pallas import tpu as pltpu
from jax.sharding import PartitionSpec as P

MESH = pl.DeviceIdType.MESH
VMEM_BYTES = 56 * 1024 * 1024
TOP = 32000.0
TINY = 1e-37
LANES = 256


def flip(value, bits):
    return sum(((value >> j) & 1) << (bits - 1 - j) for j in range(bits))


def partners_of(me, stages):
    return [me + (1 << k) * (1 - 2 * ((me // (1 << k)) % 2)) for k in range(stages)]


def gather_kernel(c_ref, g_ref, send_sem, recv_sem, *, n):
    stages = n.bit_length() - 1
    me = lax.axis_index("aux")
    partner = partners_of(me, stages)
    barrier = pltpu.get_barrier_semaphore()
    for peer in partner:
        pl.semaphore_signal(barrier, inc=1, device_id={"aux": peer}, device_id_type=MESH)
    g_ref[me] = jnp.zeros(g_ref.shape[1:], g_ref.dtype)
    g_ref[me, :, 0:c_ref.shape[0]] = c_ref[...].T
    pl.semaphore_wait(barrier, stages)

    def copy(x, k):
        unit = me + sum(partner[j] - me for j in range(stages) if (x >> j) & 1)
        return pltpu.make_async_remote_copy(
            src_ref=g_ref.at[unit], dst_ref=g_ref.at[unit], send_sem=send_sem.at[x, k], recv_sem=recv_sem.at[x ^ (1 << k)],
            device_id={"aux": partner[k]}, device_id_type=MESH)

    started = []
    for x in sorted(range(n), key=lambda x: (x.bit_count(), -x)):
        low = stages if x == 0 else (x & -x).bit_length() - 1
        if x:
            copy(x ^ (1 << low), low).wait_recv()
        for k in reversed(range(low)):
            started.append(copy(x, k))
            started[-1].start()
    for one in started:
        one.wait_send()


def slab_kernel(blocks, count, mask, t_ref, c_ref, send_ref, keep_ref, m_ref, total, factor, seen, *, width, split):
    g = pl.program_id(0)
    nb, size, _ = c_ref.shape
    slots, aux = t_ref.shape[:2]
    chunks, parts, batch, rows, cw = send_ref.shape
    group = max(d for d in range(1, 5) if width % d == 0)
    per = cw // size
    mine = lax.axis_index("aux") % 2

    @pl.when(g == 0)
    def _():
        for r in range(nb):
            seen[r] = 0
        m_ref[...] = jnp.full(m_ref.shape, TINY, m_ref.dtype)

        @pl.loop(0, slots)
        def _(q):
            pair = blocks[q]
            row, col = pair // nb, pair % nb
            live = (q < count[0]) & (mask[row, col] == 1)

            @pl.when(live)
            def _():
                part = jnp.dot(t_ref[q].reshape(aux * size, size), c_ref[col], preferred_element_type=jnp.float32)
                before = seen[row]

                @pl.when(before == 0)
                def _():
                    total[row] = part

                @pl.when(before != 0)
                def _():
                    total[row] += part

                seen[row] = 1

        @pl.loop(0, nb)
        def _(r):
            @pl.when(seen[r] != 0)
            def _():
                squares = jnp.zeros((size, LANES), jnp.float32)
                for p in range(aux):
                    rounded = total[r, p * size:(p + 1) * size].astype(jnp.bfloat16)
                    factor[r, :, p * LANES:(p + 1) * LANES] = rounded
                    wide = rounded.astype(jnp.float32)
                    squares += wide * wide
                m_ref[...] = jnp.maximum(m_ref[...], jnp.max(jnp.sum(squares, axis=1)))

            @pl.when(seen[r] == 0)
            def _():
                factor[r] = jnp.zeros(factor.shape[1:], factor.dtype)

            @pl.when(r < width - 1)
            def _():
                factor[nb + r] = factor[r]

    def fill(out_ref, first, odd, convert):
        @pl.loop(0, batch)
        def _(j):
            r = flip(first + j, nb.bit_length() - 1)

            @pl.when(seen[r] != 0)
            def _():
                for h in range(parts):
                    left = factor[r] if split == 1 else factor[r, pl.ds(pl.multiple_of((2 * h + odd) * rows, rows), rows)]
                    for d in range(0, width, group):
                        right = factor[pl.ds(r + d, group)].reshape(group * size, factor.shape[2])
                        value = convert(lax.dot_general(left, right, (((1,), (1,)), ((), ())), preferred_element_type=jnp.float32))
                        for i in range(0, group, per):
                            out_ref[(d + i) // per, flip(h, parts.bit_length() - 1), j] = value[:, i * size:(i + per) * size]

            @pl.when(seen[r] == 0)
            def _():
                for c in range(chunks):
                    for h in range(parts):
                        out_ref[c, h, j] = jnp.zeros((rows, cw), out_ref.dtype)

    inverse = 1.0 / m_ref[0:1, 0:1]
    if split == 1:
        half = nb // 2

        @pl.when(g * batch < half)
        def _():
            fill(send_ref, (1 - mine) * half + g * batch, 0, lambda value: encode(value, inverse))

        @pl.when(g * batch >= half)
        def _():
            fill(keep_ref, mine * half + g * batch - half, 0, lambda value: value)
    else:
        fill(send_ref, g * batch, 1 - mine, lambda value: encode(value, inverse))
        fill(keep_ref, g * batch, mine, lambda value: value)


def encode(value, inverse):
    root = jnp.sqrt(jnp.abs(value) * inverse) * TOP + 0.5
    return jnp.where(value < 0, -root, root).astype(jnp.int16)


def decode(code, scale):
    value = code.astype(jnp.float32)
    return value * jnp.abs(value) * scale


def reduce_kernel(first_ref, q_ref, m_ref, out_ref, acc, snd, rcv, s_m, r_m, m_snd, m_rcv, send_sem, recv_sem, sm_send, sm_recv, mir_send, mir_recv, *, n, nb, width, mirrored):
    chunks, _, rows, cw = q_ref.shape
    size = out_ref.shape[1] // nb
    per = width // chunks
    stages = n.bit_length() - 1
    me = lax.axis_index("aux")
    r = me // (n // nb)
    bit = [(me // (1 << k)) % 2 for k in range(stages)]
    partner = partners_of(me, stages)
    counts = [n >> (k + 1) for k in range(stages)]
    starts = [n - (n >> k) for k in range(stages)]
    steps = [min(4, count) for count in counts]
    mirror = list(range(1, width - 1)) if mirrored else []

    barrier = pltpu.get_barrier_semaphore()
    if mirrored:
        peers = [lax.rem(me + d, n) for d in range(1, n)]
    else:
        peers = partner
    for peer in peers:
        pl.semaphore_signal(barrier, inc=1, device_id={"aux": peer}, device_id_type=MESH)
    pl.semaphore_wait(barrier, len(peers))

    def scale_copy(k):
        return pltpu.make_async_remote_copy(
            src_ref=s_m.at[k], dst_ref=r_m.at[k], send_sem=sm_send.at[k], recv_sem=sm_recv.at[k],
            device_id={"aux": partner[k]}, device_id_type=MESH)

    def data_copy(k, c):
        span = pl.ds(starts[k], counts[k])
        return pltpu.make_async_remote_copy(
            src_ref=snd.at[c, span] if k else first_ref.at[c], dst_ref=rcv.at[c, span], send_sem=send_sem.at[k, c], recv_sem=recv_sem.at[k, c],
            device_id={"aux": partner[k]}, device_id_type=MESH)

    def mirror_copy(d):
        return pltpu.make_async_remote_copy(
            src_ref=m_snd.at[d], dst_ref=m_rcv.at[d], send_sem=mir_send.at[d], recv_sem=mir_recv.at[d],
            device_id={"aux": lax.rem(me + d, n)}, device_id_type=MESH)

    def place(block, value):
        out_ref[:, pl.ds(pl.multiple_of(block * size, size), size)] = value

    def before(k, c, j):
        return q_ref[c, pl.ds(j, steps[k])] if k == 1 else acc[c, pl.ds(j, steps[k])]

    def event(k, c):
        if k == 0:
            if c == 0:
                s_m[0] = m_ref[...]
                scale_copy(0).start()
            data_copy(0, c).start()
            return
        if c == 0:
            scale_copy(k - 1).wait_recv()
            if k < stages:
                s_m[k] = s_m[k - 1] + r_m[k - 1]
                scale_copy(k).start()
        back = r_m[k - 1, 0:1] * (1.0 / (TOP * TOP))
        data_copy(k - 1, c).wait_recv()
        if k < stages:
            inverse = 1.0 / s_m[k, 0:1]

            @pl.loop(0, counts[k], step=steps[k])
            def _(j):
                i = (1 - bit[k]) * counts[k] + j
                value = before(k, c, i) + decode(rcv[c, pl.ds(starts[k - 1] + i, steps[k])], back)
                snd[c, pl.ds(starts[k] + j, steps[k])] = encode(value, inverse)

            data_copy(k, c).start()

            @pl.loop(0, counts[k], step=steps[k])
            def _(j):
                i = bit[k] * counts[k] + j
                acc[c, pl.ds(j, steps[k])] = before(k, c, i) + decode(rcv[c, pl.ds(starts[k - 1] + i, steps[k])], back)

            return
        value = acc[c, 0] + decode(rcv[c, starts[k - 1]], back)
        for i in range(per):
            d = c * per + i
            block = value[:, i * size:(i + 1) * size]
            if d in mirror:
                m_snd[d] = block.T
                mirror_copy(d).start()
            place(lax.rem(r + d, nb), block)

    def due(k, c):
        return (0.5 * c + 1.7 * k if k < 2 else 3.2 + 2.6 * (c + 1) + 2.5 * (k - 2), k, c)

    for k, c in sorted(((k, c) for k in range(stages + 1) for c in range(chunks)), key=lambda e: due(*e)):
        event(k, c)
    for d in mirror:
        mirror_copy(d).wait_recv()
        place(lax.rem(r + nb - d, nb), m_rcv[d])
    for k in range(stages):
        scale_copy(k).wait_send()
        for c in range(chunks):
            data_copy(k, c).wait_send()
    for d in mirror:
        mirror_copy(d).wait_send()


def per_device(n, three_index, slab_blocks, slab_count, pair_mask, coeffs):
    slots, aux, size, _ = three_index.shape
    nb = pair_mask.shape[0]
    mirrored = n == nb
    split = n // nb
    width = nb // 2 + 1 if mirrored else nb
    per = 1 if mirrored else 2
    chunks, cw, rows = width // per, per * size, size // split
    stages = n.bit_length() - 1
    gathered = pl.pallas_call(
        functools.partial(gather_kernel, n=n),
        out_shape=jax.ShapeDtypeStruct((n, rows, LANES), coeffs.dtype),
        in_specs=[pl.BlockSpec(memory_space=pltpu.VMEM)],
        out_specs=pl.BlockSpec(memory_space=pltpu.VMEM),
        scratch_shapes=[pltpu.SemaphoreType.DMA((n, stages)), pltpu.SemaphoreType.DMA((n,))],
        compiler_params=pltpu.CompilerParams(collective_id=1, has_side_effects=True, vmem_limit_bytes=VMEM_BYTES),
    )(coeffs.T).reshape(nb, size, LANES)

    batch = nb // 4
    parts = max(split // 2, 1)
    shape = (chunks, parts, nb // 2 if split == 1 else nb, rows, cw)
    turns = nb // 2 // batch if split == 1 else nb // batch
    block = (chunks, parts, batch, rows, cw)
    late = turns if split == 1 else 0
    send, keep, m = pl.pallas_call(
        functools.partial(slab_kernel, width=width, split=split),
        grid_spec=pltpu.PrefetchScalarGridSpec(
            num_scalar_prefetch=3,
            grid=(nb // batch,),
            in_specs=[
                pl.BlockSpec(three_index.shape, lambda g, *_: (0, 0, 0, 0), pipeline_mode=pl.Buffered(1)),
                pl.BlockSpec((nb, size, LANES), lambda g, *_: (0, 0, 0), pipeline_mode=pl.Buffered(1)),
            ],
            out_specs=[
                pl.BlockSpec(block, lambda g, *_: (0, 0, jnp.minimum(g, turns - 1), 0, 0)),
                pl.BlockSpec(block, lambda g, *_: (0, 0, jnp.maximum(g - late, 0), 0, 0)),
                pl.BlockSpec((8, cw), lambda g, *_: (0, 0)),
            ],
            scratch_shapes=[
                pltpu.VMEM((nb, aux * size, LANES), jnp.float32),
                pltpu.VMEM((nb + width - 1, size, aux * LANES), jnp.bfloat16),
                pltpu.SMEM((nb,), jnp.int32),
            ],
        ),
        out_shape=[
            jax.ShapeDtypeStruct(shape, jnp.int16),
            jax.ShapeDtypeStruct(shape, jnp.float32),
            jax.ShapeDtypeStruct((8, cw), jnp.float32),
        ],
        compiler_params=pltpu.CompilerParams(vmem_limit_bytes=VMEM_BYTES, dimension_semantics=("arbitrary",)),
    )(slab_blocks, slab_count, pair_mask, three_index, gathered)

    return pl.pallas_call(
        functools.partial(reduce_kernel, n=n, nb=nb, width=width, mirrored=mirrored),
        out_shape=jax.ShapeDtypeStruct((rows, nb * size), jnp.float32),
        in_specs=[pl.BlockSpec(memory_space=pltpu.VMEM)] * 3,
        out_specs=pl.BlockSpec(memory_space=pltpu.VMEM),
        scratch_shapes=[
            pltpu.VMEM((chunks, n // 4, rows, cw), jnp.float32),
            pltpu.VMEM((chunks, n, rows, cw), jnp.int16),
            pltpu.VMEM((chunks, n, rows, cw), jnp.int16),
            pltpu.VMEM((stages, 8, cw), jnp.float32),
            pltpu.VMEM((stages, 8, cw), jnp.float32),
            pltpu.VMEM((width, size, size), jnp.float32),
            pltpu.VMEM((width, size, size), jnp.float32),
            pltpu.SemaphoreType.DMA((stages, chunks)),
            pltpu.SemaphoreType.DMA((stages, chunks)),
            pltpu.SemaphoreType.DMA((stages,)),
            pltpu.SemaphoreType.DMA((stages,)),
            pltpu.SemaphoreType.DMA((width,)),
            pltpu.SemaphoreType.DMA((width,)),
        ],
        compiler_params=pltpu.CompilerParams(collective_id=0, has_side_effects=True, vmem_limit_bytes=VMEM_BYTES),
    )(send.reshape(chunks, n // 2, rows, cw), keep.reshape(chunks, n // 2, rows, cw), m)


def solution(mesh):
    return jax.shard_map(
        functools.partial(per_device, mesh.shape["aux"]),
        mesh=mesh,
        in_specs=(
            P(("frag", "aux"), None, None, None),
            P(("frag", "aux")),
            P(("frag", "aux")),
            P("frag", None),
            P(("frag", "aux"), None),
        ),
        out_specs=P(("frag", "aux"), None),
        check_vma=False,
    )
```

```python
import functools

import jax
import jax.numpy as jnp
from jax import lax
from jax.experimental import pallas as pl
from jax.experimental.pallas import tpu as pltpu
from jax.sharding import PartitionSpec as P

MESH = pl.DeviceIdType.MESH
VMEM_BYTES = 56 * 1024 * 1024
TOP = 32000.0
TINY = 1e-37
LANES = 256


def flip(value, bits):
    return sum(((value >> j) & 1) << (bits - 1 - j) for j in range(bits))


def partners_of(me, stages):
    return [me + (1 << k) * (1 - 2 * ((me // (1 << k)) % 2)) for k in range(stages)]


def gather_kernel(c_ref, g_ref, send_sem, recv_sem, *, n):
    stages = n.bit_length() - 1
    me = lax.axis_index("aux")
    partner = partners_of(me, stages)
    barrier = pltpu.get_barrier_semaphore()
    for peer in partner:
        pl.semaphore_signal(barrier, inc=1, device_id={"aux": peer}, device_id_type=MESH)
    g_ref[me] = jnp.zeros(g_ref.shape[1:], g_ref.dtype)
    g_ref[me, :, 0:c_ref.shape[0]] = c_ref[...].T
    pl.semaphore_wait(barrier, stages)

    def copy(x, k):
        unit = me + sum(partner[j] - me for j in range(stages) if (x >> j) & 1)
        return pltpu.make_async_remote_copy(
            src_ref=g_ref.at[unit], dst_ref=g_ref.at[unit], send_sem=send_sem.at[x, k], recv_sem=recv_sem.at[x ^ (1 << k)],
            device_id={"aux": partner[k]}, device_id_type=MESH)

    started = []
    for x in sorted(range(n), key=lambda x: (x.bit_count(), -x)):
        low = stages if x == 0 else (x & -x).bit_length() - 1
        if x:
            copy(x ^ (1 << low), low).wait_recv()
        for k in reversed(range(low)):
            started.append(copy(x, k))
            started[-1].start()
    for one in started:
        one.wait_send()


def slab_kernel(blocks, count, mask, t_ref, c_ref, send_ref, keep_ref, m_ref, total, factor, seen, *, width, split):
    g = pl.program_id(0)
    nb, size, _ = c_ref.shape
    slots, aux = t_ref.shape[:2]
    chunks, parts, batch, rows, cw = send_ref.shape
    group = max(d for d in range(1, 5) if width % d == 0)
    per = cw // size
    mine = lax.axis_index("aux") % 2

    @pl.when(g == 0)
    def _():
        for r in range(nb):
            seen[r] = 0
        m_ref[...] = jnp.full(m_ref.shape, TINY, m_ref.dtype)

        @pl.loop(0, slots)
        def _(q):
            pair = blocks[q]
            row, col = pair // nb, pair % nb
            live = (q < count[0]) & (mask[row, col] == 1)

            @pl.when(live)
            def _():
                part = jnp.dot(t_ref[q].reshape(aux * size, size), c_ref[col], preferred_element_type=jnp.float32)
                before = seen[row]

                @pl.when(before == 0)
                def _():
                    total[row] = part

                @pl.when(before != 0)
                def _():
                    total[row] += part

                seen[row] = 1

        @pl.loop(0, nb)
        def _(r):
            @pl.when(seen[r] != 0)
            def _():
                squares = jnp.zeros((size, LANES), jnp.float32)
                for p in range(aux):
                    rounded = total[r, p * size:(p + 1) * size].astype(jnp.bfloat16)
                    factor[r, :, p * LANES:(p + 1) * LANES] = rounded
                    wide = rounded.astype(jnp.float32)
                    squares += wide * wide
                m_ref[...] = jnp.maximum(m_ref[...], jnp.max(jnp.sum(squares, axis=1)))

            @pl.when(seen[r] == 0)
            def _():
                factor[r] = jnp.zeros(factor.shape[1:], factor.dtype)

            @pl.when(r < width - 1)
            def _():
                factor[nb + r] = factor[r]

    def fill(out_ref, first, odd, convert):
        @pl.loop(0, batch)
        def _(j):
            r = flip(first + j, nb.bit_length() - 1)

            @pl.when(seen[r] != 0)
            def _():
                for h in range(parts):
                    left = factor[r] if split == 1 else factor[r, pl.ds(pl.multiple_of((2 * h + odd) * rows, rows), rows)]
                    for d in range(0, width, group):
                        right = factor[pl.ds(r + d, group)].reshape(group * size, factor.shape[2])
                        value = convert(lax.dot_general(left, right, (((1,), (1,)), ((), ())), preferred_element_type=jnp.float32))
                        for i in range(0, group, per):
                            out_ref[(d + i) // per, flip(h, parts.bit_length() - 1), j] = value[:, i * size:(i + per) * size]

            @pl.when(seen[r] == 0)
            def _():
                for c in range(chunks):
                    for h in range(parts):
                        out_ref[c, h, j] = jnp.zeros((rows, cw), out_ref.dtype)

    inverse = 1.0 / m_ref[0:1, 0:1]
    if split == 1:
        half = nb // 2

        @pl.when(g * batch < half)
        def _():
            fill(send_ref, (1 - mine) * half + g * batch, 0, lambda value: encode(value, inverse))

        @pl.when(g * batch >= half)
        def _():
            fill(keep_ref, mine * half + g * batch - half, 0, lambda value: value)
    else:
        fill(send_ref, g * batch, 1 - mine, lambda value: encode(value, inverse))
        fill(keep_ref, g * batch, mine, lambda value: value)


def encode(value, inverse):
    root = jnp.sqrt(jnp.abs(value) * inverse) * TOP + 0.5
    return jnp.where(value < 0, -root, root).astype(jnp.int16)


def decode(code, scale):
    value = code.astype(jnp.float32)
    return value * jnp.abs(value) * scale


def reduce_kernel(first_ref, q_ref, m_ref, out_ref, acc, snd, rcv, s_m, r_m, m_snd, m_rcv, send_sem, recv_sem, sm_send, sm_recv, mir_send, mir_recv, *, n, nb, width, mirrored):
    chunks, _, rows, cw = q_ref.shape
    size = out_ref.shape[1] // nb
    per = width // chunks
    stages = n.bit_length() - 1
    me = lax.axis_index("aux")
    r = me // (n // nb)
    partner = partners_of(me, stages)
    kinds = [int(stages == 4 and c % 3 == 2) for c in range(chunks)]
    orders = [list(range(stages)), [0, 2, 1, *range(3, stages)]]
    bits = [[(me // (1 << b)) % 2 for b in order] for order in orders]
    peer_of = [[partner[b] for b in order] for order in orders]
    firsts = [kinds.index(kind) for kind in sorted(set(kinds))]
    counts = [n >> (k + 1) for k in range(stages)]
    starts = [n - (n >> k) for k in range(stages)]
    steps = [min(2 if k == 1 else 4, count) for k, count in enumerate(counts)]
    mirror = list(range(1, width - 1)) if mirrored else []

    barrier = pltpu.get_barrier_semaphore()
    if mirrored:
        peers = [lax.rem(me + d, n) for d in range(1, n)]
    else:
        peers = partner
    for peer in peers:
        pl.semaphore_signal(barrier, inc=1, device_id={"aux": peer}, device_id_type=MESH)
    pl.semaphore_wait(barrier, len(peers))

    def scale_copy(kind, k):
        return pltpu.make_async_remote_copy(
            src_ref=s_m.at[kind, k], dst_ref=r_m.at[kind, k], send_sem=sm_send.at[kind, k], recv_sem=sm_recv.at[kind, k],
            device_id={"aux": peer_of[kind][k]}, device_id_type=MESH)

    def data_copy(k, c):
        span = pl.ds(starts[k], counts[k])
        return pltpu.make_async_remote_copy(
            src_ref=snd.at[c, span] if k else first_ref.at[c], dst_ref=rcv.at[c, span], send_sem=send_sem.at[k, c], recv_sem=recv_sem.at[k, c],
            device_id={"aux": peer_of[kinds[c]][k]}, device_id_type=MESH)

    def mirror_copy(d):
        return pltpu.make_async_remote_copy(
            src_ref=m_snd.at[d], dst_ref=m_rcv.at[d], send_sem=mir_send.at[d], recv_sem=mir_recv.at[d],
            device_id={"aux": lax.rem(me + d, n)}, device_id_type=MESH)

    def place(block, value):
        out_ref[:, pl.ds(pl.multiple_of(block * size, size), size)] = value

    def before(k, c, j):
        return q_ref[c, pl.ds(j, steps[k])] if k == 1 else acc[c, pl.ds(j, steps[k])]

    def at(k, c, j, side):
        if k == 1 and kinds[c]:
            half = counts[k] // 2
            return (j // half) * counts[k] + side * half + j % half
        return side * counts[k] + j

    def event(k, c):
        kind = kinds[c]
        bit = bits[kind]
        if k == 0:
            if c in firsts:
                s_m[kind, 0] = m_ref[...]
                scale_copy(kind, 0).start()
            data_copy(0, c).start()
            return
        if c in firsts:
            scale_copy(kind, k - 1).wait_recv()
            if k < stages:
                s_m[kind, k] = s_m[kind, k - 1] + r_m[kind, k - 1]
                scale_copy(kind, k).start()
        back = r_m[kind, k - 1, 0:1] * (1.0 / (TOP * TOP))
        data_copy(k - 1, c).wait_recv()
        if k < stages:
            inverse = 1.0 / s_m[kind, k, 0:1]

            @pl.loop(0, counts[k], step=steps[k])
            def _(j):
                i = at(k, c, j, 1 - bit[k])
                value = before(k, c, i) + decode(rcv[c, pl.ds(starts[k - 1] + i, steps[k])], back)
                snd[c, pl.ds(starts[k] + j, steps[k])] = encode(value, inverse)

            data_copy(k, c).start()

            @pl.loop(0, counts[k], step=steps[k])
            def _(j):
                i = at(k, c, j, bit[k])
                acc[c, pl.ds(j, steps[k])] = before(k, c, i) + decode(rcv[c, pl.ds(starts[k - 1] + i, steps[k])], back)

            return
        value = acc[c, 0] + decode(rcv[c, starts[k - 1]], back)
        for i in range(per):
            d = c * per + i
            block = value[:, i * size:(i + 1) * size]
            if d in mirror:
                m_snd[d] = block.T
                mirror_copy(d).start()
            place(lax.rem(r + d, nb), block)

    def due(k, c):
        place_in_line = sum(kind == kinds[c] for kind in kinds[:c + 1])
        return (0.5 * c + 1.7 * k if k < 2 else 3.2 + 2.6 * place_in_line + 2.5 * (k - 2), k, c)

    for k, c in sorted(((k, c) for k in range(stages + 1) for c in range(chunks)), key=lambda e: due(*e)):
        event(k, c)
    for d in mirror:
        mirror_copy(d).wait_recv()
        place(lax.rem(r + nb - d, nb), m_rcv[d])
    for k in range(stages):
        for first in firsts:
            scale_copy(kinds[first], k).wait_send()
        for c in range(chunks):
            data_copy(k, c).wait_send()
    for d in mirror:
        mirror_copy(d).wait_send()


def per_device(n, three_index, slab_blocks, slab_count, pair_mask, coeffs):
    slots, aux, size, _ = three_index.shape
    nb = pair_mask.shape[0]
    mirrored = n == nb
    split = n // nb
    width = nb // 2 + 1 if mirrored else nb
    per = 1 if mirrored else 2
    chunks, cw, rows = width // per, per * size, size // split
    stages = n.bit_length() - 1
    gathered = pl.pallas_call(
        functools.partial(gather_kernel, n=n),
        out_shape=jax.ShapeDtypeStruct((n, rows, LANES), coeffs.dtype),
        in_specs=[pl.BlockSpec(memory_space=pltpu.VMEM)],
        out_specs=pl.BlockSpec(memory_space=pltpu.VMEM),
        scratch_shapes=[pltpu.SemaphoreType.DMA((n, stages)), pltpu.SemaphoreType.DMA((n,))],
        compiler_params=pltpu.CompilerParams(collective_id=1, has_side_effects=True, vmem_limit_bytes=VMEM_BYTES),
    )(coeffs.T).reshape(nb, size, LANES)

    batch = nb // 4
    parts = max(split // 2, 1)
    shape = (chunks, parts, nb // 2 if split == 1 else nb, rows, cw)
    turns = nb // 2 // batch if split == 1 else nb // batch
    block = (chunks, parts, batch, rows, cw)
    late = turns if split == 1 else 0
    send, keep, m = pl.pallas_call(
        functools.partial(slab_kernel, width=width, split=split),
        grid_spec=pltpu.PrefetchScalarGridSpec(
            num_scalar_prefetch=3,
            grid=(nb // batch,),
            in_specs=[
                pl.BlockSpec(three_index.shape, lambda g, *_: (0, 0, 0, 0), pipeline_mode=pl.Buffered(1)),
                pl.BlockSpec((nb, size, LANES), lambda g, *_: (0, 0, 0), pipeline_mode=pl.Buffered(1)),
            ],
            out_specs=[
                pl.BlockSpec(block, lambda g, *_: (0, 0, jnp.minimum(g, turns - 1), 0, 0)),
                pl.BlockSpec(block, lambda g, *_: (0, 0, jnp.maximum(g - late, 0), 0, 0)),
                pl.BlockSpec((8, cw), lambda g, *_: (0, 0)),
            ],
            scratch_shapes=[
                pltpu.VMEM((nb, aux * size, LANES), jnp.float32),
                pltpu.VMEM((nb + width - 1, size, aux * LANES), jnp.bfloat16),
                pltpu.SMEM((nb,), jnp.int32),
            ],
        ),
        out_shape=[
            jax.ShapeDtypeStruct(shape, jnp.int16),
            jax.ShapeDtypeStruct(shape, jnp.float32),
            jax.ShapeDtypeStruct((8, cw), jnp.float32),
        ],
        compiler_params=pltpu.CompilerParams(vmem_limit_bytes=VMEM_BYTES, dimension_semantics=("arbitrary",)),
    )(slab_blocks, slab_count, pair_mask, three_index, gathered)

    return pl.pallas_call(
        functools.partial(reduce_kernel, n=n, nb=nb, width=width, mirrored=mirrored),
        out_shape=jax.ShapeDtypeStruct((rows, nb * size), jnp.float32),
        in_specs=[pl.BlockSpec(memory_space=pltpu.VMEM)] * 3,
        out_specs=pl.BlockSpec(memory_space=pltpu.VMEM),
        scratch_shapes=[
            pltpu.VMEM((chunks, n // 4, rows, cw), jnp.float32),
            pltpu.VMEM((chunks, n, rows, cw), jnp.int16),
            pltpu.VMEM((chunks, n, rows, cw), jnp.int16),
            pltpu.VMEM((2, stages, 8, cw), jnp.float32),
            pltpu.VMEM((2, stages, 8, cw), jnp.float32),
            pltpu.VMEM((width, size, size), jnp.float32),
            pltpu.VMEM((width, size, size), jnp.float32),
            pltpu.SemaphoreType.DMA((stages, chunks)),
            pltpu.SemaphoreType.DMA((stages, chunks)),
            pltpu.SemaphoreType.DMA((2, stages)),
            pltpu.SemaphoreType.DMA((2, stages)),
            pltpu.SemaphoreType.DMA((width,)),
            pltpu.SemaphoreType.DMA((width,)),
        ],
        compiler_params=pltpu.CompilerParams(collective_id=0, has_side_effects=True, vmem_limit_bytes=VMEM_BYTES),
    )(send.reshape(chunks, n // 2, rows, cw), keep.reshape(chunks, n // 2, rows, cw), m)


def solution(mesh):
    return jax.shard_map(
        functools.partial(per_device, mesh.shape["aux"]),
        mesh=mesh,
        in_specs=(
            P(("frag", "aux"), None, None, None),
            P(("frag", "aux")),
            P(("frag", "aux")),
            P("frag", None),
            P(("frag", "aux"), None),
        ),
        out_specs=P(("frag", "aux"), None),
        check_vma=False,
    )
```

```python
import functools

import jax
import jax.numpy as jnp
from jax import lax
from jax.experimental import pallas as pl
from jax.experimental.pallas import tpu as pltpu
from jax.sharding import PartitionSpec as P

MESH = pl.DeviceIdType.MESH
VMEM_BYTES = 56 * 1024 * 1024
TOP = 32000.0
TINY = 1e-28
LANES = 256


def flip(value, bits):
    return sum(((value >> j) & 1) << (bits - 1 - j) for j in range(bits))


def partners_of(me, stages):
    return [me + (1 << k) * (1 - 2 * ((me // (1 << k)) % 2)) for k in range(stages)]


def gather_kernel(c_ref, g_ref, send_sem, recv_sem, *, n):
    stages = n.bit_length() - 1
    me = lax.axis_index("aux")
    partner = partners_of(me, stages)
    barrier = pltpu.get_barrier_semaphore()
    for peer in partner:
        pl.semaphore_signal(barrier, inc=1, device_id={"aux": peer}, device_id_type=MESH)
    g_ref[me] = jnp.zeros(g_ref.shape[1:], g_ref.dtype)
    g_ref[me, :, 0:c_ref.shape[0]] = c_ref[...].T
    pl.semaphore_wait(barrier, stages)

    def copy(x, k):
        unit = me + sum(partner[j] - me for j in range(stages) if (x >> j) & 1)
        return pltpu.make_async_remote_copy(
            src_ref=g_ref.at[unit], dst_ref=g_ref.at[unit], send_sem=send_sem.at[x, k], recv_sem=recv_sem.at[x ^ (1 << k)],
            device_id={"aux": partner[k]}, device_id_type=MESH)

    started = []
    for x in sorted(range(n), key=lambda x: (x.bit_count(), -x)):
        low = stages if x == 0 else (x & -x).bit_length() - 1
        if x:
            copy(x ^ (1 << low), low).wait_recv()
        for k in reversed(range(low)):
            started.append(copy(x, k))
            started[-1].start()
    for one in started:
        one.wait_send()


def slab_kernel(blocks, count, mask, t_ref, c_ref, send_ref, keep_ref, m_ref, total, factor, seen, *, width, split):
    g = pl.program_id(0)
    nb, size, _ = c_ref.shape
    slots, aux = t_ref.shape[:2]
    chunks, parts, batch, rows, cw = send_ref.shape
    group = max(d for d in range(1, 5) if width % d == 0)
    per = cw // size
    mine = lax.axis_index("aux") % 2

    @pl.when(g == 0)
    def _():
        for r in range(nb):
            seen[r] = 0
        m_ref[...] = jnp.full(m_ref.shape, TINY, m_ref.dtype)

        @pl.loop(0, slots)
        def _(q):
            pair = blocks[q]
            row, col = pair // nb, pair % nb
            live = (q < count[0]) & (mask[row, col] == 1)

            @pl.when(live)
            def _():
                part = jnp.dot(t_ref[q].reshape(aux * size, size), c_ref[col], preferred_element_type=jnp.float32)
                before = seen[row]

                @pl.when(before == 0)
                def _():
                    total[row] = part

                @pl.when(before != 0)
                def _():
                    total[row] += part

                seen[row] = 1

        @pl.loop(0, nb)
        def _(r):
            @pl.when(seen[r] != 0)
            def _():
                squares = jnp.zeros((size, LANES), jnp.float32)
                for p in range(aux):
                    rounded = total[r, p * size:(p + 1) * size].astype(jnp.bfloat16)
                    factor[r, :, p * LANES:(p + 1) * LANES] = rounded
                    wide = rounded.astype(jnp.float32)
                    squares += wide * wide
                m_ref[...] = jnp.maximum(m_ref[...], jnp.max(jnp.sum(squares, axis=1)))

            @pl.when(seen[r] == 0)
            def _():
                factor[r] = jnp.zeros(factor.shape[1:], factor.dtype)

            @pl.when(r < width - 1)
            def _():
                factor[nb + r] = factor[r]

    def fill(out_ref, first, odd, convert):
        @pl.loop(0, batch)
        def _(j):
            r = flip(first + j, nb.bit_length() - 1)

            @pl.when(seen[r] != 0)
            def _():
                for h in range(parts):
                    left = factor[r] if split == 1 else factor[r, pl.ds(pl.multiple_of((2 * h + odd) * rows, rows), rows)]
                    for d in range(0, width, group):
                        right = factor[pl.ds(r + d, group)].reshape(group * size, factor.shape[2])
                        value = convert(lax.dot_general(left, right, (((1,), (1,)), ((), ())), preferred_element_type=jnp.float32))
                        for i in range(0, group, per):
                            out_ref[(d + i) // per, flip(h, parts.bit_length() - 1), j] = value[:, i * size:(i + per) * size]

            @pl.when(seen[r] == 0)
            def _():
                for c in range(chunks):
                    for h in range(parts):
                        out_ref[c, h, j] = jnp.zeros((rows, cw), out_ref.dtype)

    inverse = 1.0 / m_ref[0:1, 0:1]
    if split == 1:
        half = nb // 2

        @pl.when(g * batch < half)
        def _():
            fill(send_ref, (1 - mine) * half + g * batch, 0, lambda value: encode(value, inverse))

        @pl.when(g * batch >= half)
        def _():
            fill(keep_ref, mine * half + g * batch - half, 0, lambda value: value)
    else:
        fill(send_ref, g * batch, 1 - mine, lambda value: encode(value, inverse))
        fill(keep_ref, g * batch, mine, lambda value: value)


def encode(value, inverse):
    scaled = value * (inverse * (TOP * TOP))
    root = scaled * lax.rsqrt(jnp.abs(scaled) + 1e-20)
    return (root + jnp.where(scaled < 0, -0.5, 0.5)).astype(jnp.int16)


def decode(code, scale):
    value = code.astype(jnp.float32)
    return value * jnp.abs(value) * scale


def reduce_kernel(first_ref, q_ref, m_ref, out_ref, acc, snd, rcv, s_m, r_m, m_snd, m_rcv, send_sem, recv_sem, sm_send, sm_recv, mir_send, mir_recv, *, n, nb, width, mirrored):
    chunks, _, rows, cw = q_ref.shape
    size = out_ref.shape[1] // nb
    per = width // chunks
    stages = n.bit_length() - 1
    me = lax.axis_index("aux")
    r = me // (n // nb)
    bit = [(me // (1 << k)) % 2 for k in range(stages)]
    partner = partners_of(me, stages)
    counts = [n >> (k + 1) for k in range(stages)]
    starts = [n - (n >> k) for k in range(stages)]
    steps = [min(4, count) for count in counts]
    mirror = list(range(1, width - 1)) if mirrored else []

    barrier = pltpu.get_barrier_semaphore()
    if mirrored:
        peers = [lax.rem(me + d, n) for d in range(1, n)]
    else:
        peers = partner
    for peer in peers:
        pl.semaphore_signal(barrier, inc=1, device_id={"aux": peer}, device_id_type=MESH)
    pl.semaphore_wait(barrier, len(peers))

    def scale_copy(k):
        return pltpu.make_async_remote_copy(
            src_ref=s_m.at[k], dst_ref=r_m.at[k], send_sem=sm_send.at[k], recv_sem=sm_recv.at[k],
            device_id={"aux": partner[k]}, device_id_type=MESH)

    def data_copy(k, c):
        span = pl.ds(starts[k], counts[k])
        return pltpu.make_async_remote_copy(
            src_ref=snd.at[c, span] if k else first_ref.at[c], dst_ref=rcv.at[c, span], send_sem=send_sem.at[k, c], recv_sem=recv_sem.at[k, c],
            device_id={"aux": partner[k]}, device_id_type=MESH)

    def mirror_copy(d):
        return pltpu.make_async_remote_copy(
            src_ref=m_snd.at[d], dst_ref=m_rcv.at[d], send_sem=mir_send.at[d], recv_sem=mir_recv.at[d],
            device_id={"aux": lax.rem(me + d, n)}, device_id_type=MESH)

    def place(block, value):
        out_ref[:, pl.ds(pl.multiple_of(block * size, size), size)] = value

    def before(k, c, j):
        return q_ref[c, pl.ds(j, steps[k])] if k == 1 else acc[c, pl.ds(j, steps[k])]

    def event(k, c):
        if k == 0:
            if c == 0:
                s_m[0] = m_ref[...]
                scale_copy(0).start()
            data_copy(0, c).start()
            return
        if c == 0:
            scale_copy(k - 1).wait_recv()
            if k < stages:
                s_m[k] = s_m[k - 1] + r_m[k - 1]
                scale_copy(k).start()
        back = r_m[k - 1, 0:1] * (1.0 / (TOP * TOP))
        data_copy(k - 1, c).wait_recv()
        if k < stages:
            inverse = 1.0 / s_m[k, 0:1]

            @pl.loop(0, counts[k], step=steps[k])
            def _(j):
                i = (1 - bit[k]) * counts[k] + j
                value = before(k, c, i) + decode(rcv[c, pl.ds(starts[k - 1] + i, steps[k])], back)
                snd[c, pl.ds(starts[k] + j, steps[k])] = encode(value, inverse)

            data_copy(k, c).start()

            @pl.loop(0, counts[k], step=steps[k])
            def _(j):
                i = bit[k] * counts[k] + j
                acc[c, pl.ds(j, steps[k])] = before(k, c, i) + decode(rcv[c, pl.ds(starts[k - 1] + i, steps[k])], back)

            return
        value = acc[c, 0] + decode(rcv[c, starts[k - 1]], back)
        for i in range(per):
            d = c * per + i
            block = value[:, i * size:(i + 1) * size]
            if d in mirror:
                m_snd[d] = block.T
                mirror_copy(d).start()
            place(lax.rem(r + d, nb), block)

    def due(k, c):
        return (0.5 * c + 1.7 * k if k < 2 else 3.2 + 2.6 * (c + 1) + 2.5 * (k - 2), k, c)

    for k, c in sorted(((k, c) for k in range(stages + 1) for c in range(chunks)), key=lambda e: due(*e)):
        event(k, c)
    for d in mirror:
        mirror_copy(d).wait_recv()
        place(lax.rem(r + nb - d, nb), m_rcv[d])
    for k in range(stages):
        scale_copy(k).wait_send()
        for c in range(chunks):
            data_copy(k, c).wait_send()
    for d in mirror:
        mirror_copy(d).wait_send()


def per_device(n, three_index, slab_blocks, slab_count, pair_mask, coeffs):
    slots, aux, size, _ = three_index.shape
    nb = pair_mask.shape[0]
    mirrored = n == nb
    split = n // nb
    width = nb // 2 + 1 if mirrored else nb
    per = 1 if mirrored else 2
    chunks, cw, rows = width // per, per * size, size // split
    stages = n.bit_length() - 1
    gathered = pl.pallas_call(
        functools.partial(gather_kernel, n=n),
        out_shape=jax.ShapeDtypeStruct((n, rows, LANES), coeffs.dtype),
        in_specs=[pl.BlockSpec(memory_space=pltpu.VMEM)],
        out_specs=pl.BlockSpec(memory_space=pltpu.VMEM),
        scratch_shapes=[pltpu.SemaphoreType.DMA((n, stages)), pltpu.SemaphoreType.DMA((n,))],
        compiler_params=pltpu.CompilerParams(collective_id=1, has_side_effects=True, vmem_limit_bytes=VMEM_BYTES),
    )(coeffs.T).reshape(nb, size, LANES)

    batch = nb // 4
    parts = max(split // 2, 1)
    shape = (chunks, parts, nb // 2 if split == 1 else nb, rows, cw)
    turns = nb // 2 // batch if split == 1 else nb // batch
    block = (chunks, parts, batch, rows, cw)
    late = turns if split == 1 else 0
    send, keep, m = pl.pallas_call(
        functools.partial(slab_kernel, width=width, split=split),
        grid_spec=pltpu.PrefetchScalarGridSpec(
            num_scalar_prefetch=3,
            grid=(nb // batch,),
            in_specs=[
                pl.BlockSpec(three_index.shape, lambda g, *_: (0, 0, 0, 0), pipeline_mode=pl.Buffered(1)),
                pl.BlockSpec((nb, size, LANES), lambda g, *_: (0, 0, 0), pipeline_mode=pl.Buffered(1)),
            ],
            out_specs=[
                pl.BlockSpec(block, lambda g, *_: (0, 0, jnp.minimum(g, turns - 1), 0, 0)),
                pl.BlockSpec(block, lambda g, *_: (0, 0, jnp.maximum(g - late, 0), 0, 0)),
                pl.BlockSpec((8, cw), lambda g, *_: (0, 0)),
            ],
            scratch_shapes=[
                pltpu.VMEM((nb, aux * size, LANES), jnp.float32),
                pltpu.VMEM((nb + width - 1, size, aux * LANES), jnp.bfloat16),
                pltpu.SMEM((nb,), jnp.int32),
            ],
        ),
        out_shape=[
            jax.ShapeDtypeStruct(shape, jnp.int16),
            jax.ShapeDtypeStruct(shape, jnp.float32),
            jax.ShapeDtypeStruct((8, cw), jnp.float32),
        ],
        compiler_params=pltpu.CompilerParams(vmem_limit_bytes=VMEM_BYTES, dimension_semantics=("arbitrary",)),
    )(slab_blocks, slab_count, pair_mask, three_index, gathered)

    return pl.pallas_call(
        functools.partial(reduce_kernel, n=n, nb=nb, width=width, mirrored=mirrored),
        out_shape=jax.ShapeDtypeStruct((rows, nb * size), jnp.float32),
        in_specs=[pl.BlockSpec(memory_space=pltpu.VMEM)] * 3,
        out_specs=pl.BlockSpec(memory_space=pltpu.VMEM),
        scratch_shapes=[
            pltpu.VMEM((chunks, n // 4, rows, cw), jnp.float32),
            pltpu.VMEM((chunks, n, rows, cw), jnp.int16),
            pltpu.VMEM((chunks, n, rows, cw), jnp.int16),
            pltpu.VMEM((stages, 8, cw), jnp.float32),
            pltpu.VMEM((stages, 8, cw), jnp.float32),
            pltpu.VMEM((width, size, size), jnp.float32),
            pltpu.VMEM((width, size, size), jnp.float32),
            pltpu.SemaphoreType.DMA((stages, chunks)),
            pltpu.SemaphoreType.DMA((stages, chunks)),
            pltpu.SemaphoreType.DMA((stages,)),
            pltpu.SemaphoreType.DMA((stages,)),
            pltpu.SemaphoreType.DMA((width,)),
            pltpu.SemaphoreType.DMA((width,)),
        ],
        compiler_params=pltpu.CompilerParams(collective_id=0, has_side_effects=True, vmem_limit_bytes=VMEM_BYTES),
    )(send.reshape(chunks, n // 2, rows, cw), keep.reshape(chunks, n // 2, rows, cw), m)


def solution(mesh):
    return jax.shard_map(
        functools.partial(per_device, mesh.shape["aux"]),
        mesh=mesh,
        in_specs=(
            P(("frag", "aux"), None, None, None),
            P(("frag", "aux")),
            P(("frag", "aux")),
            P("frag", None),
            P(("frag", "aux"), None),
        ),
        out_specs=P(("frag", "aux"), None),
        check_vma=False,
    )
```

```python
import functools

import jax
import jax.numpy as jnp
from jax import lax
from jax.experimental import pallas as pl
from jax.experimental.pallas import tpu as pltpu
from jax.sharding import PartitionSpec as P

MESH = pl.DeviceIdType.MESH
VMEM_BYTES = 56 * 1024 * 1024
TOP = 32000.0
TINY = 1e-28
LANES = 256


def flip(value, bits):
    return sum(((value >> j) & 1) << (bits - 1 - j) for j in range(bits))


def partners_of(me, stages):
    return [me + (1 << k) * (1 - 2 * ((me // (1 << k)) % 2)) for k in range(stages)]


def gather_kernel(c_ref, g_ref, send_sem, recv_sem, *, n):
    stages = n.bit_length() - 1
    me = lax.axis_index("aux")
    partner = partners_of(me, stages)
    barrier = pltpu.get_barrier_semaphore()
    for peer in partner:
        pl.semaphore_signal(barrier, inc=1, device_id={"aux": peer}, device_id_type=MESH)
    g_ref[me] = jnp.zeros(g_ref.shape[1:], g_ref.dtype)
    g_ref[me, :, 0:c_ref.shape[0]] = c_ref[...].T
    pl.semaphore_wait(barrier, stages)

    def copy(x, k):
        unit = me + sum(partner[j] - me for j in range(stages) if (x >> j) & 1)
        return pltpu.make_async_remote_copy(
            src_ref=g_ref.at[unit], dst_ref=g_ref.at[unit], send_sem=send_sem.at[x, k], recv_sem=recv_sem.at[x ^ (1 << k)],
            device_id={"aux": partner[k]}, device_id_type=MESH)

    started = []
    for x in sorted(range(n), key=lambda x: (x.bit_count(), -x)):
        low = stages if x == 0 else (x & -x).bit_length() - 1
        if x:
            copy(x ^ (1 << low), low).wait_recv()
        for k in reversed(range(low)):
            started.append(copy(x, k))
            started[-1].start()
    for one in started:
        one.wait_send()


def slab_kernel(blocks, count, mask, t_ref, c_ref, send_ref, keep_ref, m_ref, total, factor, seen, *, width, split):
    g = pl.program_id(0)
    nb, size, _ = c_ref.shape
    slots, aux = t_ref.shape[:2]
    chunks, parts, batch, rows, cw = send_ref.shape
    group = max(d for d in range(1, 10) if width % d == 0)
    per = cw // size
    mine = lax.axis_index("aux") % 2

    @pl.when(g == 0)
    def _():
        for r in range(nb):
            seen[r] = 0
        m_ref[...] = jnp.full(m_ref.shape, TINY, m_ref.dtype)

        @pl.loop(0, slots)
        def _(q):
            pair = blocks[q]
            row, col = pair // nb, pair % nb
            live = (q < count[0]) & (mask[row, col] == 1)

            @pl.when(live)
            def _():
                part = jnp.dot(t_ref[q].reshape(aux * size, size), c_ref[col], preferred_element_type=jnp.float32)
                before = seen[row]

                @pl.when(before == 0)
                def _():
                    total[row] = part

                @pl.when(before != 0)
                def _():
                    total[row] += part

                seen[row] = 1

        @pl.loop(0, nb)
        def _(r):
            @pl.when(seen[r] != 0)
            def _():
                squares = jnp.zeros((size, LANES), jnp.float32)
                for p in range(aux):
                    rounded = total[r, p * size:(p + 1) * size].astype(jnp.bfloat16)
                    factor[r, :, p * LANES:(p + 1) * LANES] = rounded
                    wide = rounded.astype(jnp.float32)
                    squares += wide * wide
                m_ref[...] = jnp.maximum(m_ref[...], jnp.max(jnp.sum(squares, axis=1)))

            @pl.when(seen[r] == 0)
            def _():
                factor[r] = jnp.zeros(factor.shape[1:], factor.dtype)

            @pl.when(r < width - 1)
            def _():
                factor[nb + r] = factor[r]

    def fill(out_ref, first, odd, convert):
        @pl.loop(0, batch)
        def _(j):
            r = flip(first + j, nb.bit_length() - 1)

            @pl.when(seen[r] != 0)
            def _():
                for h in range(parts):
                    left = factor[r] if split == 1 else factor[r, pl.ds(pl.multiple_of((2 * h + odd) * rows, rows), rows)]
                    for d in range(0, width, group):
                        right = factor[pl.ds(r + d, group)].reshape(group * size, factor.shape[2])
                        value = convert(lax.dot_general(left, right, (((1,), (1,)), ((), ())), preferred_element_type=jnp.float32))
                        for i in range(0, group, per):
                            out_ref[(d + i) // per, flip(h, parts.bit_length() - 1), j] = value[:, i * size:(i + per) * size]

            @pl.when(seen[r] == 0)
            def _():
                for c in range(chunks):
                    for h in range(parts):
                        out_ref[c, h, j] = jnp.zeros((rows, cw), out_ref.dtype)

    inverse = 1.0 / m_ref[0:1, 0:1]
    if split == 1:
        half = nb // 2

        @pl.when(g * batch < half)
        def _():
            fill(send_ref, (1 - mine) * half + g * batch, 0, lambda value: encode(value, inverse))

        @pl.when(g * batch >= half)
        def _():
            fill(keep_ref, mine * half + g * batch - half, 0, lambda value: value)
    else:
        fill(send_ref, g * batch, 1 - mine, lambda value: encode(value, inverse))
        fill(keep_ref, g * batch, mine, lambda value: value)


def encode(value, inverse):
    scaled = value * (inverse * (TOP * TOP))
    root = scaled * lax.rsqrt(jnp.abs(scaled) + 1e-20)
    return (root + jnp.where(scaled < 0, -0.5, 0.5)).astype(jnp.int16)


def decode(code, scale):
    value = code.astype(jnp.float32)
    return value * jnp.abs(value) * scale


def reduce_kernel(first_ref, q_ref, m_ref, out_ref, acc, snd, rcv, s_m, r_m, m_snd, m_rcv, send_sem, recv_sem, sm_send, sm_recv, mir_send, mir_recv, *, n, nb, width, mirrored):
    chunks, _, rows, cw = q_ref.shape
    size = out_ref.shape[1] // nb
    per = width // chunks
    stages = n.bit_length() - 1
    me = lax.axis_index("aux")
    r = me // (n // nb)
    bit = [(me // (1 << k)) % 2 for k in range(stages)]
    partner = partners_of(me, stages)
    counts = [n >> (k + 1) for k in range(stages)]
    starts = [n - (n >> k) for k in range(stages)]
    steps = [min(4, count) for count in counts]
    mirror = list(range(1, width - 1)) if mirrored else []

    barrier = pltpu.get_barrier_semaphore()
    if mirrored:
        peers = [lax.rem(me + d, n) for d in range(1, n)]
    else:
        peers = partner
    for peer in peers:
        pl.semaphore_signal(barrier, inc=1, device_id={"aux": peer}, device_id_type=MESH)
    pl.semaphore_wait(barrier, len(peers))

    def scale_copy(k):
        return pltpu.make_async_remote_copy(
            src_ref=s_m.at[k], dst_ref=r_m.at[k], send_sem=sm_send.at[k], recv_sem=sm_recv.at[k],
            device_id={"aux": partner[k]}, device_id_type=MESH)

    def data_copy(k, c):
        span = pl.ds(starts[k], counts[k])
        return pltpu.make_async_remote_copy(
            src_ref=snd.at[c, span] if k else first_ref.at[c], dst_ref=rcv.at[c, span], send_sem=send_sem.at[k, c], recv_sem=recv_sem.at[k, c],
            device_id={"aux": partner[k]}, device_id_type=MESH)

    def mirror_copy(d):
        return pltpu.make_async_remote_copy(
            src_ref=m_snd.at[d], dst_ref=m_rcv.at[d], send_sem=mir_send.at[d], recv_sem=mir_recv.at[d],
            device_id={"aux": lax.rem(me + d, n)}, device_id_type=MESH)

    def place(block, value):
        out_ref[:, pl.ds(pl.multiple_of(block * size, size), size)] = value

    def before(k, c, j):
        return q_ref[c, pl.ds(j, steps[k])] if k == 1 else acc[c, pl.ds(j, steps[k])]

    def event(k, c):
        if k == 0:
            if c == 0:
                s_m[0] = m_ref[...]
                scale_copy(0).start()
            data_copy(0, c).start()
            return
        if c == 0:
            scale_copy(k - 1).wait_recv()
            if k < stages:
                s_m[k] = s_m[k - 1] + r_m[k - 1]
                scale_copy(k).start()
        back = r_m[k - 1, 0:1] * (1.0 / (TOP * TOP))
        data_copy(k - 1, c).wait_recv()
        if k < stages:
            inverse = 1.0 / s_m[k, 0:1]

            @pl.loop(0, counts[k], step=steps[k])
            def _(j):
                i = (1 - bit[k]) * counts[k] + j
                value = before(k, c, i) + decode(rcv[c, pl.ds(starts[k - 1] + i, steps[k])], back)
                snd[c, pl.ds(starts[k] + j, steps[k])] = encode(value, inverse)

            data_copy(k, c).start()

            @pl.loop(0, counts[k], step=steps[k])
            def _(j):
                i = bit[k] * counts[k] + j
                acc[c, pl.ds(j, steps[k])] = before(k, c, i) + decode(rcv[c, pl.ds(starts[k - 1] + i, steps[k])], back)

            return
        value = acc[c, 0] + decode(rcv[c, starts[k - 1]], back)
        for i in range(per):
            d = c * per + i
            block = value[:, i * size:(i + 1) * size]
            if d in mirror:
                m_snd[d] = block.T
                mirror_copy(d).start()
            place(lax.rem(r + d, nb), block)

    def due(k, c):
        return (0.5 * c + 1.7 * k if k < 2 else 3.2 + 2.6 * (c + 1) + 2.5 * (k - 2), k, c)

    for k, c in sorted(((k, c) for k in range(stages + 1) for c in range(chunks)), key=lambda e: due(*e)):
        event(k, c)
    for d in mirror:
        mirror_copy(d).wait_recv()
        place(lax.rem(r + nb - d, nb), m_rcv[d])
    for k in range(stages):
        scale_copy(k).wait_send()
        for c in range(chunks):
            data_copy(k, c).wait_send()
    for d in mirror:
        mirror_copy(d).wait_send()


def per_device(n, three_index, slab_blocks, slab_count, pair_mask, coeffs):
    slots, aux, size, _ = three_index.shape
    nb = pair_mask.shape[0]
    mirrored = n == nb
    split = n // nb
    width = nb // 2 + 1 if mirrored else nb
    per = 1 if mirrored else 2
    chunks, cw, rows = width // per, per * size, size // split
    stages = n.bit_length() - 1
    gathered = pl.pallas_call(
        functools.partial(gather_kernel, n=n),
        out_shape=jax.ShapeDtypeStruct((n, rows, LANES), coeffs.dtype),
        in_specs=[pl.BlockSpec(memory_space=pltpu.VMEM)],
        out_specs=pl.BlockSpec(memory_space=pltpu.VMEM),
        scratch_shapes=[pltpu.SemaphoreType.DMA((n, stages)), pltpu.SemaphoreType.DMA((n,))],
        compiler_params=pltpu.CompilerParams(collective_id=1, has_side_effects=True, vmem_limit_bytes=VMEM_BYTES),
    )(coeffs.T).reshape(nb, size, LANES)

    batch = nb // 4
    parts = max(split // 2, 1)
    shape = (chunks, parts, nb // 2 if split == 1 else nb, rows, cw)
    turns = nb // 2 // batch if split == 1 else nb // batch
    block = (chunks, parts, batch, rows, cw)
    late = turns if split == 1 else 0
    send, keep, m = pl.pallas_call(
        functools.partial(slab_kernel, width=width, split=split),
        grid_spec=pltpu.PrefetchScalarGridSpec(
            num_scalar_prefetch=3,
            grid=(nb // batch,),
            in_specs=[
                pl.BlockSpec(three_index.shape, lambda g, *_: (0, 0, 0, 0), pipeline_mode=pl.Buffered(1)),
                pl.BlockSpec((nb, size, LANES), lambda g, *_: (0, 0, 0), pipeline_mode=pl.Buffered(1)),
            ],
            out_specs=[
                pl.BlockSpec(block, lambda g, *_: (0, 0, jnp.minimum(g, turns - 1), 0, 0)),
                pl.BlockSpec(block, lambda g, *_: (0, 0, jnp.maximum(g - late, 0), 0, 0)),
                pl.BlockSpec((8, cw), lambda g, *_: (0, 0)),
            ],
            scratch_shapes=[
                pltpu.VMEM((nb, aux * size, LANES), jnp.float32),
                pltpu.VMEM((nb + width - 1, size, aux * LANES), jnp.bfloat16),
                pltpu.SMEM((nb,), jnp.int32),
            ],
        ),
        out_shape=[
            jax.ShapeDtypeStruct(shape, jnp.int16),
            jax.ShapeDtypeStruct(shape, jnp.float32),
            jax.ShapeDtypeStruct((8, cw), jnp.float32),
        ],
        compiler_params=pltpu.CompilerParams(vmem_limit_bytes=VMEM_BYTES, dimension_semantics=("arbitrary",)),
    )(slab_blocks, slab_count, pair_mask, three_index, gathered)

    return pl.pallas_call(
        functools.partial(reduce_kernel, n=n, nb=nb, width=width, mirrored=mirrored),
        out_shape=jax.ShapeDtypeStruct((rows, nb * size), jnp.float32),
        in_specs=[pl.BlockSpec(memory_space=pltpu.VMEM)] * 3,
        out_specs=pl.BlockSpec(memory_space=pltpu.VMEM),
        scratch_shapes=[
            pltpu.VMEM((chunks, n // 4, rows, cw), jnp.float32),
            pltpu.VMEM((chunks, n, rows, cw), jnp.int16),
            pltpu.VMEM((chunks, n, rows, cw), jnp.int16),
            pltpu.VMEM((stages, 8, cw), jnp.float32),
            pltpu.VMEM((stages, 8, cw), jnp.float32),
            pltpu.VMEM((width, size, size), jnp.float32),
            pltpu.VMEM((width, size, size), jnp.float32),
            pltpu.SemaphoreType.DMA((stages, chunks)),
            pltpu.SemaphoreType.DMA((stages, chunks)),
            pltpu.SemaphoreType.DMA((stages,)),
            pltpu.SemaphoreType.DMA((stages,)),
            pltpu.SemaphoreType.DMA((width,)),
            pltpu.SemaphoreType.DMA((width,)),
        ],
        compiler_params=pltpu.CompilerParams(collective_id=0, has_side_effects=True, vmem_limit_bytes=VMEM_BYTES),
    )(send.reshape(chunks, n // 2, rows, cw), keep.reshape(chunks, n // 2, rows, cw), m)


def solution(mesh):
    return jax.shard_map(
        functools.partial(per_device, mesh.shape["aux"]),
        mesh=mesh,
        in_specs=(
            P(("frag", "aux"), None, None, None),
            P(("frag", "aux")),
            P(("frag", "aux")),
            P("frag", None),
            P(("frag", "aux"), None),
        ),
        out_specs=P(("frag", "aux"), None),
        check_vma=False,
    )
```
